128 devices in a mesh: group: 8 (over x, z_lo), seq: 16 (over z_hi, y, core).
Axes of the slice: x: 4, y: 4, z: 4 (z_hi: 2, z_lo: 2; z = z_hi * 2 + z_lo), core: 2. Of those that a mesh axis runs over, the one named last changes fastest.
Arguments:
- queries: bfloat16 [576, 24576], P(None, 'seq'), may hold values from -13 to 13
- prefix_latent: bfloat16 [8192, 576], P(('group', 'seq')), may hold values from -6 to 6
- tail_latent: bfloat16 [576, 256, 576], P('group', 'seq'), may hold values from -6 to 6
- tail_length: int32 [576], P('group'), may hold values from 1 to 256, 73728 in all
- slot_request: int32 [576], P('group'), may hold values from 0 to 575, each once
- key_absorb: bfloat16 [128, 128, 512], P('seq'), may hold values from -0.5 to 0.5
- value_up: bfloat16 [128, 512, 128], P('seq'), may hold values from -0.25 to 0.25
- out_proj: bfloat16 [16384, 7168], P('seq'), may hold values from -0.75 to 0.75
Outputs:
- mixed: bfloat16 [576, 7168], P('group', 'seq')
The draws below stay inside these ranges and needn't reach their ends.
All inputs are finite; a program needn't handle non-finite values. No bound on the sum of `tail_length` on one device may be relied on, other than what follows from the above.
Results may differ from the reference program's by a relative error of at most 0.02.
Values may be sent and summed in bfloat16 or wider, within the bound.
No kernel may reach another device: no remote copies, remote signals or barrier semaphores. Data moves between devices by JAX's collectives and lax.ppermute only.
A program may use at most 192 MiB of HBM per device.

```python
import math
import jax
import jax.numpy as jnp
import numpy as np
from jax import lax

D = 7168
H = 128
DL = 512
DR = 64
DN = 128
DV = 128
PREFIX = 8192
TAIL = 256
REQS = 576


def draw_queries(key, part):
    key = jax.random.fold_in(key, 11)
    values = jnp.clip(jax.random.normal(key, (REQS, H, DN + DR), jnp.float32), -6.0, 6.0)
    return values.reshape(REQS, H * (DN + DR)).astype(jnp.bfloat16)


def draw_prefix_latent(key, part):
    key = jax.random.fold_in(key, 23)
    values = jnp.clip(jax.random.normal(key, (PREFIX, DL + DR), jnp.float32), -6.0, 6.0)
    return values.astype(jnp.bfloat16)


def level_of(rng, shape, cuts, smallest, largest):
    level = 1.0
    for axis_at, shards_of in cuts:
        heights = jax.random.uniform(jax.random.fold_in(jax.random.fold_in(rng, 6), axis_at), (shards_of,), jnp.float32, smallest / len(cuts), largest / len(cuts))
        level = level * jnp.repeat(jnp.exp(heights), shape[axis_at] // shards_of).reshape((-1,) + (1,) * (len(shape) - 1 - axis_at))
    return level


def split_up(amount, total, reach, skew):
    loads = [(1 << 20) // math.isqrt(rank ** skew) + 1 for rank in range(2, amount + 1)]
    surplus, given = total - reach - (amount - 1), [1] * (amount - 1)
    while surplus > 0:
        candidates = [i for i in range(amount - 1) if given[i] < reach]
        mass, left = sum([loads[i] for i in candidates]), surplus
        for i in candidates:
            extra = min(reach - given[i], max(1, left * loads[i] // mass), surplus)
            given[i] = given[i] + extra
            surplus = surplus - extra
    return np.array([reach] + given)


def ragged(key, count, total, limit, slope):
    if count == 2:
        one = jax.random.randint(key, (), max(1, total - limit), min(limit, total - 1) + 1)
        return jnp.stack([one, total - one])
    tallies = jnp.asarray(split_up(count, total, limit, slope), jnp.int32)
    couples = (count - 1) // 2
    donor, taker = tallies[1:1 + 2 * couples:2], tallies[2:2 + 2 * couples:2]
    room = jnp.minimum(donor - 1, limit - taker)
    shifted = jax.random.randint(jax.random.fold_in(key, 1), (couples,), 0, 1 << 20) % (room + 1)
    tallies = tallies.at[1:1 + 2 * couples:2].set(donor - shifted).at[2:2 + 2 * couples:2].set(taker + shifted)
    return tallies[jax.random.permutation(jax.random.fold_in(key, 2), count)]


def bell_draw(rng, dims, width, most, split=(), kind=jnp.bfloat16):
    entries = jax.random.normal(rng, dims, jnp.float32) * width
    if len(split) > 0:
        entries = level_of(rng, dims, split, -0.22, 0.18) * entries
    return jnp.clip(entries, min=-most, max=most).astype(kind)


def setup_inputs(seed: int = 0) -> dict:
    key_of = jax.random.split(jax.random.key(seed), 9)
    return {
        "queries": draw_queries(jax.random.fold_in(key_of[8], 71), 0),
        "prefix_latent": draw_prefix_latent(jax.random.fold_in(key_of[8], 71), 0),
        "tail_latent": bell_draw(key_of[2], (REQS, TAIL, DL + DR), 1.0, 6.0, ((0, 8), (1, 16))),
        "tail_length": ragged(key_of[3], REQS, REQS * TAIL // 2, TAIL, 2).astype(jnp.int32),
        "slot_request": jax.random.permutation(key_of[4], REQS).astype(jnp.int32),
        "key_absorb": bell_draw(key_of[5], (H, DN, DL), DN ** -0.5, 0.5, ((0, 16),)),
        "value_up": bell_draw(key_of[6], (H, DL, DV), DL ** -0.5, 0.25, ((0, 16),)),
        "out_proj": bell_draw(key_of[7], (H * DV, D), 64 ** -0.5, 0.75, ((0, 16),)),
    }


def reference(queries, prefix_latent, tail_latent, tail_length, slot_request, key_absorb, value_up, out_proj):
    picked = queries[slot_request].reshape(REQS, H, DN + DR)
    query_latent = jnp.einsum('rhn,hnl->rhl', picked[:, :, :DN].astype(jnp.float32), key_absorb.astype(jnp.float32)).astype(jnp.bfloat16)
    query_full = jnp.concatenate([query_latent, picked[:, :, DN:]], axis=2)
    score_scale = 1.0 / math.sqrt(DN + DR)
    prefix_usable = jnp.arange(PREFIX, dtype=jnp.int32) >= 0

    def attend(operands):
        query_row, tail_rows, length = operands
        keys = jnp.concatenate([prefix_latent, tail_rows], axis=0)
        scores = jnp.dot(query_row, keys.T, preferred_element_type=jnp.float32) * score_scale
        usable = jnp.concatenate([prefix_usable, jnp.arange(TAIL, dtype=jnp.int32) < length])
        masked = jnp.where(usable[None, :], scores, -jnp.inf)
        highest = lax.optimization_barrier(jnp.max(masked, axis=1, keepdims=True))
        weights = jnp.where(usable[None, :], jnp.exp(masked - highest), 0.0)
        weight_sum = lax.optimization_barrier(jnp.sum(weights, axis=1, keepdims=True))
        context_sum = jnp.dot(weights.astype(jnp.bfloat16), keys[:, :DL], preferred_element_type=jnp.float32)
        return (context_sum / weight_sum).astype(jnp.bfloat16)
    context = lax.map(attend, (query_full, tail_latent, tail_length))
    head_out = jnp.einsum('rhl,hlv->rhv', context.astype(jnp.float32), value_up.astype(jnp.float32)).astype(jnp.bfloat16)
    head_out = head_out.reshape(REQS, H * DV)
    return jnp.dot(head_out, out_proj, preferred_element_type=jnp.float32).astype(jnp.bfloat16)
```

```python
import functools
import math

import jax
import jax.numpy as jnp
from jax import lax
from jax.experimental import pallas as pl
from jax.experimental.pallas import tpu as pltpu
from jax.sharding import Mesh, PartitionSpec as P

ROW_BLOCK = 192


def attend_kernel(
    first, last, width, exponent_scale, key_count, q_ref, *refs
):
    key_refs = refs[:key_count]
    refs = refs[key_count:]
    q = q_ref[...]
    scores = [
        lax.dot_general(
            q, k_ref[...], (((1,), (1,)), ((), ())), preferred_element_type=jnp.float32
        )
        for k_ref in key_refs
    ]
    highest = functools.reduce(
        jnp.maximum, [jnp.max(s, axis=1, keepdims=True) for s in scores]
    )
    if not first:
        stat_ref, acc_ref = refs[:2]
        refs = refs[2:]
        old_highest = stat_ref[:, 0:1]
        old_sum = stat_ref[:, 128:129]
        highest = jnp.maximum(highest, old_highest)
        fade = jnp.exp2((old_highest - highest) * exponent_scale)
    weight_sum = None
    acc = None
    for s, k_ref in zip(scores, key_refs):
        w = jnp.exp2((s - highest) * exponent_scale)
        part_sum = jnp.sum(w, axis=1, keepdims=True)
        part = jnp.dot(
            w.astype(jnp.bfloat16), k_ref[:, :width], preferred_element_type=jnp.float32
        )
        weight_sum = part_sum if weight_sum is None else weight_sum + part_sum
        acc = part if acc is None else acc + part
    if not first:
        weight_sum = weight_sum + old_sum * fade
        acc = acc + acc_ref[...] * fade
    if not last:
        out_stat_ref, out_acc_ref = refs
        out_stat_ref[:, :128] = jnp.broadcast_to(highest, (q.shape[0], 128))
        out_stat_ref[:, 128:] = jnp.broadcast_to(weight_sum, (q.shape[0], 128))
        out_acc_ref[...] = acc
    else:
        (out_ref,) = refs
        pack_context(out_ref, acc, weight_sum, highest, exponent_scale, width)


def pack_context(out_ref, acc, weight_sum, highest, exponent_scale, width):
    rows = acc.shape[0]
    out_ref[:, :width] = (acc / weight_sum).astype(jnp.bfloat16)
    level = highest * exponent_scale + jnp.log2(weight_sum)
    high = level.astype(jnp.bfloat16)
    rest = level - high.astype(jnp.float32)
    middle = rest.astype(jnp.bfloat16)
    low = rest - middle.astype(jnp.float32)
    lane = lax.broadcasted_iota(jnp.int32, (rows, 128), 1)
    packed = jnp.where(
        lane == 0,
        high.astype(jnp.float32),
        jnp.where(lane == 1, middle.astype(jnp.float32), jnp.where(lane == 2, low, 0.0)),
    )
    out_ref[:, width:] = packed.astype(jnp.bfloat16)


def attend(q, keys, state, last, width, exponent_scale):
    rows, features = q.shape
    first = state is None
    row_map = lambda i: (i, 0)
    all_map = lambda i: (0, 0)
    in_specs = [pl.BlockSpec((ROW_BLOCK, features), row_map)]
    in_specs += [pl.BlockSpec(k.shape, all_map) for k in keys]
    args = [q, *keys]
    if not first:
        in_specs += [
            pl.BlockSpec((ROW_BLOCK, 256), row_map),
            pl.BlockSpec((ROW_BLOCK, width), row_map),
        ]
        args += list(state)
    if last:
        out_shape = jax.ShapeDtypeStruct((rows, width + 128), jnp.bfloat16)
        out_specs = pl.BlockSpec((ROW_BLOCK, width + 128), row_map)
    else:
        out_shape = (
            jax.ShapeDtypeStruct((rows, 256), jnp.float32),
            jax.ShapeDtypeStruct((rows, width), jnp.float32),
        )
        out_specs = (
            pl.BlockSpec((ROW_BLOCK, 256), row_map),
            pl.BlockSpec((ROW_BLOCK, width), row_map),
        )
    key_rows = sum(k.shape[0] for k in keys)
    return pl.pallas_call(
        functools.partial(attend_kernel, first, last, width, exponent_scale, len(keys)),
        grid=(rows // ROW_BLOCK,),
        in_specs=in_specs,
        out_specs=out_specs,
        out_shape=out_shape,
        compiler_params=pltpu.CompilerParams(vmem_limit_bytes=32 * 1024 * 1024),
        cost_estimate=pl.CostEstimate(
            flops=2 * rows * key_rows * (features + width),
            bytes_accessed=2 * rows * features + 2 * key_rows * features,
            transcendentals=rows * key_rows,
        ),
        name="prefix_attend",
    )(*args)


def tail_kernel(width, exponent_scale, length_ref, core_ref, q_ref, own_ref, other_ref, out_ref):
    slot = pl.program_id(0)
    sources, _, heads, features = q_ref.shape
    span = own_ref.shape[2]
    q = q_ref[...].reshape(sources * heads, features)
    length = length_ref[slot]
    core = core_ref[0]
    parts = []
    for ref, side in ((own_ref, core), (other_ref, 1 - core)):
        keys = ref[...].reshape(sources * span, features)
        s = lax.dot_general(
            q, keys, (((1,), (1,)), ((), ())), preferred_element_type=jnp.float32
        )
        t = lax.broadcasted_iota(jnp.int32, s.shape, 1)
        position = (t // span) * (2 * span) + side * span + t % span
        parts.append((jnp.where(position < length, s, -1e30), position < length, keys))
    highest = functools.reduce(
        jnp.maximum, [jnp.max(s, axis=1, keepdims=True) for s, _, _ in parts]
    )
    weight_sum = 0.0
    acc = 0.0
    for s, usable, keys in parts:
        w = jnp.where(usable, jnp.exp2((s - highest) * exponent_scale), 0.0)
        weight_sum = weight_sum + jnp.sum(w, axis=1, keepdims=True)
        acc = acc + jnp.dot(
            w.astype(jnp.bfloat16), keys[:, :width], preferred_element_type=jnp.float32
        )
    pack_tail(out_ref, acc, weight_sum, highest, exponent_scale, width, sources, heads)


def pack_tail(out_ref, acc, weight_sum, highest, exponent_scale, width, sources, heads):
    rows = sources * heads
    context = (acc / weight_sum).astype(jnp.bfloat16)
    level = highest * exponent_scale + jnp.log2(weight_sum)
    high = level.astype(jnp.bfloat16)
    rest = level - high.astype(jnp.float32)
    middle = rest.astype(jnp.bfloat16)
    low = rest - middle.astype(jnp.float32)
    lane = lax.broadcasted_iota(jnp.int32, (rows, 128), 1)
    packed = jnp.where(
        lane == 0,
        high.astype(jnp.float32),
        jnp.where(lane == 1, middle.astype(jnp.float32), jnp.where(lane == 2, low, 0.0)),
    ).astype(jnp.bfloat16)
    out_ref[:, 0, :, :width] = context.reshape(sources, heads, width)
    out_ref[:, 0, :, width:] = packed.reshape(sources, heads, 128)


def attend_tails(q, own, other, length, core, width, exponent_scale):
    sources, slots, heads, features = q.shape
    span = own.shape[2]
    block = lambda last2, last1: pl.BlockSpec(
        (sources, 1, last2, last1), lambda i, *_: (0, i, 0, 0)
    )
    return pl.pallas_call(
        functools.partial(tail_kernel, width, exponent_scale),
        grid_spec=pltpu.PrefetchScalarGridSpec(
            num_scalar_prefetch=2,
            grid=(slots,),
            in_specs=[block(heads, features), block(span, features), block(span, features)],
            out_specs=block(heads, width + 128),
        ),
        out_shape=jax.ShapeDtypeStruct((sources, slots, heads, width + 128), jnp.bfloat16),
        compiler_params=pltpu.CompilerParams(vmem_limit_bytes=32 * 1024 * 1024),
        cost_estimate=pl.CostEstimate(
            flops=2 * slots * sources * heads * sources * 2 * span * (features + width),
            bytes_accessed=2 * (q.size + own.size + other.size),
            transcendentals=slots * sources * heads * sources * 2 * span,
        ),
        name="tail_attend",
    )(length, core, q, own, other)


def on_device(
    queries, prefix_latent, tail_latent, tail_length, slot_request, key_absorb, value_up, out_proj
):
    heads_here, nope_width, latent_width = key_absorb.shape
    value_width = value_up.shape[2]
    req_rows = slot_request.shape[0]
    features = prefix_latent.shape[1]
    rope_width = features - latent_width
    exponent_scale = math.log2(math.e) / math.sqrt(nope_width + rope_width)
    core = lax.axis_index("core")
    chips = lax.axis_size("z_hi") * lax.axis_size("y")
    chip = lax.axis_index("z_hi") * lax.axis_size("y") + lax.axis_index("y")
    slots = req_rows // chips

    def ring(value, axis, by):
        size = lax.axis_size(axis)
        return lax.ppermute(value, axis, [(i, (i + by) % size) for i in range(size)])

    def other_core(value):
        return lax.ppermute(value, "core", [(0, 1), (1, 0)])

    def z_ring(value, by):
        low, high = lax.axis_size("z_lo"), lax.axis_size("z_hi")
        size = low * high
        place = lambda z: (z % low) * high + z // low
        pairs = [(place(z), place((z + by) % size)) for z in range(size)]
        return lax.ppermute(value, ("z_lo", "z_hi"), pairs)

    def exchange(value):
        return lax.all_to_all(value, ("z_hi", "y"), 0, 0, tiled=True)

    held = jnp.concatenate(
        [prefix_latent] + [ring(prefix_latent, "y", by) for by in (1, -1, 2)], axis=0
    )
    held = jnp.concatenate([held] + [z_ring(held, by) for by in (1, -1, 2)], axis=0)

    picked = jnp.take(queries, slot_request, axis=0).reshape(
        req_rows, heads_here, nope_width + rope_width
    )
    query_latent = jnp.einsum(
        "rhn,hnl->rhl", picked[:, :, :nope_width], key_absorb, preferred_element_type=jnp.float32
    ).astype(jnp.bfloat16)
    query_full = jnp.concatenate([query_latent, picked[:, :, nope_width:]], axis=2)

    tail_own = exchange(tail_latent).reshape(chips, slots, *tail_latent.shape[1:])
    tail_query = exchange(query_full).reshape(chips, slots, heads_here, features)
    tail_other = other_core(tail_own)
    length = lax.dynamic_slice_in_dim(tail_length, chip * slots, slots)
    tail_part = attend_tails(
        tail_query, tail_own, tail_other, length, core.reshape(1), latent_width, exponent_scale
    )
    tail_part = exchange(
        tail_part.reshape(chips * slots, heads_here, latent_width + 128)
    )

    query_rows = query_full.reshape(req_rows * heads_here, features)
    both = jnp.concatenate([query_rows, other_core(query_rows)], axis=0)
    half = held.shape[0] // 2
    right, left = ring(held, "x", 1), ring(held, "x", -1)
    far_a, far_b = ring(held[:half], "x", 2), ring(held[half:], "x", 2)
    state = attend(both, [held], None, False, latent_width, exponent_scale)
    state = attend(both, [right, left], state, False, latent_width, exponent_scale)
    packed = attend(both, [far_a, far_b], state, True, latent_width, exponent_scale)
    received = other_core(packed[query_rows.shape[0] :])

    parts = [
        part.reshape(req_rows, heads_here, latent_width + 128)
        for part in (packed[: query_rows.shape[0]], received, tail_part)
    ]
    levels = [
        jnp.sum(part[:, :, latent_width : latent_width + 3].astype(jnp.float32), axis=2)
        for part in parts
    ]
    top = functools.reduce(jnp.maximum, levels)
    shares = [jnp.exp2(level - top) for level in levels]
    total = shares[0] + shares[1] + shares[2]
    context = sum(
        part[:, :, :latent_width].astype(jnp.float32) * (share / total)[:, :, None]
        for part, share in zip(parts, shares)
    ).astype(jnp.bfloat16)
    head_out = jnp.einsum(
        "rhl,hlv->rhv", context, value_up, preferred_element_type=jnp.float32
    ).astype(jnp.bfloat16)
    head_out = head_out.reshape(req_rows, heads_here * value_width)
    mixed = jnp.dot(head_out, out_proj, preferred_element_type=jnp.float32)
    width_here = out_proj.shape[1] // (2 * chips)
    mixed = mixed.astype(jnp.bfloat16).reshape(req_rows, chips, 2, width_here)
    mixed = mixed.transpose(2, 1, 0, 3)
    keep = lax.dynamic_index_in_dim(mixed, core, 0, False)
    give = lax.dynamic_index_in_dim(mixed, 1 - core, 0, False)
    paired = keep.astype(jnp.float32) + other_core(give).astype(jnp.float32)
    gathered = exchange(paired.astype(jnp.bfloat16))
    return jnp.sum(gathered.astype(jnp.float32), axis=0).astype(jnp.bfloat16)


def solution(mesh):
    fine = Mesh(
        mesh.devices.reshape(4, 2, 2, 4, 2), ("x", "z_lo", "z_hi", "y", "core")
    )
    group, seq = ("x", "z_lo"), ("z_hi", "y", "core")
    placed = (
        P(None, seq),
        P(group + seq, None),
        P(group, seq, None),
        P(group),
        P(group),
        P(seq, None, None),
        P(seq, None, None),
        P(seq, None),
    )
    return jax.shard_map(
        on_device, mesh=fine, in_specs=placed, out_specs=P(group, seq), check_vma=False
    )
```

```python
import functools
import math

import jax
import jax.numpy as jnp
from jax import lax
from jax.experimental import pallas as pl
from jax.experimental.pallas import tpu as pltpu
from jax.sharding import Mesh, PartitionSpec as P

ROW_BLOCK = 288
KEY_BLOCK = 512
SLOT_BLOCK = 3
VMEM = 58 * 1024 * 1024
COST = pl.CostEstimate(flops=1000000, bytes_accessed=1000000, transcendentals=0)


def pack(acc, weight_sum, highest, exponent_scale):
    context = (acc / weight_sum).astype(jnp.bfloat16)
    level = highest * exponent_scale + jnp.log2(weight_sum)
    high = level.astype(jnp.bfloat16).astype(jnp.float32)
    middle = (level - high).astype(jnp.bfloat16).astype(jnp.float32)
    low = level - high - middle
    lane = lax.broadcasted_iota(jnp.int32, (acc.shape[0], 128), 1)
    terms = jnp.where(
        lane == 0, high, jnp.where(lane == 1, middle, jnp.where(lane == 2, low, 0.0))
    )
    return context, terms.astype(jnp.bfloat16)


def attend_kernel(first, last, width, exponent_scale, key_count, q_ref, *refs):
    key_refs = refs[:key_count]
    refs = refs[key_count:]
    q = q_ref[...]
    if first:
        highest = weight_sum = acc = None
    else:
        stat_ref, acc_ref = refs[:2]
        refs = refs[2:]
        highest = stat_ref[:, 0:1]
        weight_sum = stat_ref[:, 128:129]
        acc = acc_ref[...]
    blocks = [
        (k_ref, at) for k_ref in key_refs for at in range(0, k_ref.shape[1], KEY_BLOCK)
    ]

    def scores_of(block):
        k_ref, at = block
        return jnp.dot(
            q, k_ref[:, at : at + KEY_BLOCK], preferred_element_type=jnp.float32
        )

    scores = scores_of(blocks[0])
    for place, (k_ref, at) in enumerate(blocks):
        upcoming = scores_of(blocks[place + 1]) if place + 1 < len(blocks) else None
        block_highest = jnp.max(scores, axis=1, keepdims=True)
        new_highest = (
            block_highest if highest is None else jnp.maximum(highest, block_highest)
        )
        w = jnp.exp2((scores - new_highest) * exponent_scale)
        part_sum = jnp.sum(w, axis=1, keepdims=True)
        part = lax.dot_general(
            w.astype(jnp.bfloat16),
            k_ref[:width, at : at + KEY_BLOCK],
            (((1,), (1,)), ((), ())),
            preferred_element_type=jnp.float32,
        )
        if highest is None:
            weight_sum, acc = part_sum, part
        else:
            fade = jnp.exp2((highest - new_highest) * exponent_scale)
            weight_sum = weight_sum * fade + part_sum
            acc = acc * fade + part
        highest, scores = new_highest, upcoming
    if last:
        (out_ref,) = refs
        out_ref[:, :width], out_ref[:, width:] = pack(acc, weight_sum, highest, exponent_scale)
    else:
        out_stat_ref, out_acc_ref = refs
        out_stat_ref[:, :128] = jnp.broadcast_to(highest, (q.shape[0], 128))
        out_stat_ref[:, 128:] = jnp.broadcast_to(weight_sum, (q.shape[0], 128))
        out_acc_ref[...] = acc


def attend(q, keys, state, last, width, exponent_scale, second=False):
    rows, features = q.shape
    first = state is None
    row_map = lambda i: (i, 0)
    all_map = lambda i: (0, 0)
    in_specs = [pl.BlockSpec((ROW_BLOCK, features), row_map)]
    in_specs += [pl.BlockSpec(k.shape, all_map) for k in keys]
    args = [q, *keys]
    state_specs = (
        pl.BlockSpec((ROW_BLOCK, 256), row_map),
        pl.BlockSpec((ROW_BLOCK, width), row_map),
    )
    skip = rows // ROW_BLOCK if second else 0
    old_map = lambda i: (i + skip, 0)
    if not first:
        in_specs += [
            pl.BlockSpec((ROW_BLOCK, 256), old_map),
            pl.BlockSpec((ROW_BLOCK, width), old_map),
        ]
        args += list(state)
    if last:
        out_shape = jax.ShapeDtypeStruct((rows, width + 128), jnp.bfloat16)
        out_specs = pl.BlockSpec((ROW_BLOCK, width + 128), row_map)
    else:
        out_shape = (
            jax.ShapeDtypeStruct((rows, 256), jnp.float32),
            jax.ShapeDtypeStruct((rows, width), jnp.float32),
        )
        out_specs = state_specs
    return pl.pallas_call(
        functools.partial(attend_kernel, first, last, width, exponent_scale, len(keys)),
        grid=(rows // ROW_BLOCK,),
        in_specs=in_specs,
        out_specs=out_specs,
        out_shape=out_shape,
        compiler_params=pltpu.CompilerParams(vmem_limit_bytes=VMEM),
        cost_estimate=COST,
        name="prefix_attend",
    )(*args)


def tail_kernel(width, exponent_scale, length_ref, core_ref, q_ref, own_ref, other_ref, out_ref):
    first_slot = pl.program_id(0) * SLOT_BLOCK
    sources, _, heads, features = q_ref.shape
    span = own_ref.shape[2]
    core = core_ref[0]
    for at in range(SLOT_BLOCK):
        q = q_ref[:, at].reshape(sources * heads, features)
        length = length_ref[first_slot + at]
        parts = []
        for ref, side in ((own_ref, core), (other_ref, 1 - core)):
            keys = ref[:, at].reshape(sources * span, features)
            s = lax.dot_general(
                q, keys, (((1,), (1,)), ((), ())), preferred_element_type=jnp.float32
            )
            t = lax.broadcasted_iota(jnp.int32, s.shape, 1)
            usable = (t // span) * (2 * span) + side * span + t % span < length
            parts.append((jnp.where(usable, s, -1e30), usable, keys))
        highest = functools.reduce(
            jnp.maximum, [jnp.max(s, axis=1, keepdims=True) for s, _, _ in parts]
        )
        weight_sum = 0.0
        acc = 0.0
        for s, usable, keys in parts:
            w = jnp.where(usable, jnp.exp2((s - highest) * exponent_scale), 0.0)
            weight_sum = weight_sum + jnp.sum(w, axis=1, keepdims=True)
            acc = acc + jnp.dot(
                w.astype(jnp.bfloat16), keys[:, :width], preferred_element_type=jnp.float32
            )
        context, level = pack(acc, weight_sum, highest, exponent_scale)
        out_ref[:, at, :, :width] = context.reshape(sources, heads, width)
        out_ref[:, at, :, width:] = level.reshape(sources, heads, 128)


def attend_tails(q, own, other, length, core, width, exponent_scale):
    sources, slots, heads, features = q.shape
    span = own.shape[2]
    block = lambda last2, last1: pl.BlockSpec(
        (sources, SLOT_BLOCK, last2, last1), lambda i, *_: (0, i, 0, 0)
    )
    return pl.pallas_call(
        functools.partial(tail_kernel, width, exponent_scale),
        grid_spec=pltpu.PrefetchScalarGridSpec(
            num_scalar_prefetch=2,
            grid=(slots // SLOT_BLOCK,),
            in_specs=[block(heads, features), block(span, features), block(span, features)],
            out_specs=block(heads, width + 128),
        ),
        out_shape=jax.ShapeDtypeStruct((sources, slots, heads, width + 128), jnp.bfloat16),
        compiler_params=pltpu.CompilerParams(vmem_limit_bytes=VMEM),
        cost_estimate=COST,
        name="tail_attend",
    )(length, core, q, own, other)


def finish_kernel(
    width, core_ref, own_ref, received_ref, tail_ref, up_ref, proj_ref,
    keep_ref, give_ref, context_ref, head_ref,
):
    heads = up_ref.shape[0]
    value_width = up_ref.shape[2]
    req_rows = head_ref.shape[0]

    @pl.when(pl.program_id(0) == 0)
    def _():
        refs = (own_ref, received_ref, tail_ref)
        levels = [
            jnp.sum(ref[:, width:].astype(jnp.float32), axis=1, keepdims=True) for ref in refs
        ]
        top = functools.reduce(jnp.maximum, levels)
        shares = [jnp.exp2(level - top) for level in levels]
        total = shares[0] + shares[1] + shares[2]
        context = sum(
            ref[:, :width].astype(jnp.float32) * (share / total)
            for ref, share in zip(refs, shares)
        )
        context_ref[...] = context.reshape(req_rows, heads, width)
        for h in range(heads):
            head_ref[:, h * value_width : (h + 1) * value_width] = jnp.dot(
                context_ref[:, h, :].astype(jnp.bfloat16),
                up_ref[h],
                preferred_element_type=jnp.float32,
            ).astype(jnp.bfloat16)

    mixed = jnp.dot(head_ref[...], proj_ref[...], preferred_element_type=jnp.float32)
    mixed = mixed.astype(jnp.bfloat16)
    half = mixed.shape[1] // 2
    early = core_ref[0] == 0
    keep_ref[0] = jnp.where(early, mixed[:, :half], mixed[:, half:])
    give_ref[0] = jnp.where(early, mixed[:, half:], mixed[:, :half])


def finish(own, received, tail, value_up, out_proj, core, chips):
    heads, width, value_width = value_up.shape
    rows, packed_width = own.shape
    req_rows = rows // heads
    depth, columns = out_proj.shape
    block = columns // chips
    half = jax.ShapeDtypeStruct((chips, req_rows, block // 2), jnp.bfloat16)
    half_spec = pl.BlockSpec((1, req_rows, block // 2), lambda i, *_: (i, 0, 0))
    whole = pl.BlockSpec((rows, packed_width), lambda i, *_: (0, 0))
    return pl.pallas_call(
        functools.partial(finish_kernel, width),
        grid_spec=pltpu.PrefetchScalarGridSpec(
            num_scalar_prefetch=1,
            grid=(chips,),
            in_specs=[
                whole,
                whole,
                whole,
                pl.BlockSpec(value_up.shape, lambda i, *_: (0, 0, 0)),
                pl.BlockSpec((depth, block), lambda i, *_: (0, i)),
            ],
            out_specs=(half_spec, half_spec),
            scratch_shapes=[
                pltpu.VMEM((req_rows, heads, width), jnp.float32),
                pltpu.VMEM((req_rows, heads * value_width), jnp.bfloat16),
            ],
        ),
        out_shape=(half, half),
        compiler_params=pltpu.CompilerParams(vmem_limit_bytes=VMEM),
        cost_estimate=COST,
        name="finish",
    )(core, own, received, tail, value_up, out_proj)


def on_device(
    queries, prefix_latent, tail_latent, tail_length, slot_request, key_absorb, value_up, out_proj
):
    heads_here, nope_width, latent_width = key_absorb.shape
    value_width = value_up.shape[2]
    req_rows = slot_request.shape[0]
    features = prefix_latent.shape[1]
    rope_width = features - latent_width
    exponent_scale = math.log2(math.e) / math.sqrt(nope_width + rope_width)
    core = lax.axis_index("core")
    chips = lax.axis_size("z_hi") * lax.axis_size("y")
    chip = lax.axis_index("z_hi") * lax.axis_size("y") + lax.axis_index("y")
    slots = req_rows // chips

    def ring(value, axis, by):
        size = lax.axis_size(axis)
        return lax.ppermute(value, axis, [(i, (i + by) % size) for i in range(size)])

    def other_core(value):
        return lax.ppermute(value, "core", [(0, 1), (1, 0)])

    def z_ring(value, by):
        low, high = lax.axis_size("z_lo"), lax.axis_size("z_hi")
        size = low * high
        place = lambda z: (z % low) * high + z // low
        pairs = [(place(z), place((z + by) % size)) for z in range(size)]
        return lax.ppermute(value, ("z_lo", "z_hi"), pairs)

    def exchange(value):
        return lax.all_to_all(value, ("z_hi", "y"), 0, 0, tiled=True)

    picked = jnp.take(queries, slot_request, axis=0).reshape(
        req_rows, heads_here, nope_width + rope_width
    )
    query_latent = jnp.einsum(
        "rhn,hnl->rhl", picked[:, :, :nope_width], key_absorb, preferred_element_type=jnp.float32
    ).astype(jnp.bfloat16)
    query_full = jnp.concatenate([query_latent, picked[:, :, nope_width:]], axis=2)
    query_rows = query_full.reshape(req_rows * heads_here, features)

    held = jnp.concatenate(
        [prefix_latent] + [ring(prefix_latent, "y", by) for by in (1, -1, 2)], axis=0
    ).T
    shifted = [z_ring(held, by) for by in (1, -1, 2)]
    held = jnp.concatenate([held] + shifted, axis=1)
    tail_query = exchange(query_full).reshape(chips, slots, heads_here, features)
    query_other = other_core(query_rows)
    both = jnp.concatenate([query_rows, query_other], axis=0)
    tail_latent, both, _, tail_query = lax.optimization_barrier(
        (tail_latent, both, held, tail_query)
    )

    half = held.shape[1] // 2
    right, left = ring(held, "x", 1), ring(held, "x", -1)
    far = [ring(held[:, :half], "x", 2), ring(held[:, half:], "x", 2)]

    tail_own = exchange(tail_latent).reshape(chips, slots, *tail_latent.shape[1:])
    length = lax.dynamic_slice_in_dim(tail_length, chip * slots, slots)
    core_at = core.reshape(1)

    go = functools.partial(attend, width=latent_width, exponent_scale=exponent_scale)
    state = go(both, [held], None, False)
    tail_own, state, right, left = lax.optimization_barrier((tail_own, state, right, left))
    tail_other = other_core(tail_own)

    tail_part = attend_tails(
        tail_query, tail_own, tail_other, length, core_at, latent_width, exponent_scale
    )
    tail_part, right, left = lax.optimization_barrier((tail_part, right, left))
    tail_part = exchange(
        tail_part.reshape(chips * slots, heads_here, latent_width + 128)
    ).reshape(req_rows * heads_here, latent_width + 128)

    state = go(both, [right, left], state, False)
    state, far, tail_part = lax.optimization_barrier((state, far, tail_part))
    packed_other = go(query_other, far, state, True, second=True)
    received = other_core(packed_other)
    packed_own = go(query_rows, far, state, True)

    keep, give = finish(
        packed_own, received, tail_part, value_up, out_proj, core_at, chips
    )
    paired = keep.astype(jnp.float32) + other_core(give).astype(jnp.float32)
    gathered = exchange(paired.astype(jnp.bfloat16))
    return jnp.sum(gathered.astype(jnp.float32), axis=0).astype(jnp.bfloat16)


def solution(mesh):
    fine = Mesh(
        mesh.devices.reshape(4, 2, 2, 4, 2), ("x", "z_lo", "z_hi", "y", "core")
    )
    group, seq = ("x", "z_lo"), ("z_hi", "y", "core")
    placed = (
        P(None, seq),
        P(group + seq, None),
        P(group, seq, None),
        P(group),
        P(group),
        P(seq, None, None),
        P(seq, None, None),
        P(seq, None),
    )
    return jax.shard_map(
        on_device, mesh=fine, in_specs=placed, out_specs=P(group, seq), check_vma=False
    )
```

```python
import functools
import math

import jax
import jax.numpy as jnp
from jax import lax
from jax.experimental import pallas as pl
from jax.experimental.pallas import tpu as pltpu
from jax.sharding import Mesh, PartitionSpec as P

ROW_BLOCK = 288
KEY_BLOCK = 512
VMEM = 58 * 1024 * 1024
COST = pl.CostEstimate(flops=10**11, bytes_accessed=10**8, transcendentals=0)


def pack(acc, weight_sum, highest, exponent_scale):
    context = (acc / weight_sum).astype(jnp.bfloat16)
    level = highest * exponent_scale + jnp.log2(weight_sum)
    high = level.astype(jnp.bfloat16).astype(jnp.float32)
    middle = (level - high).astype(jnp.bfloat16).astype(jnp.float32)
    low = level - high - middle
    lane = lax.broadcasted_iota(jnp.int32, (acc.shape[0], 128), 1)
    terms = jnp.where(
        lane == 0, high, jnp.where(lane == 1, middle, jnp.where(lane == 2, low, 0.0))
    )
    return context, terms.astype(jnp.bfloat16)


def attend_kernel(first, last, width, exponent_scale, key_count, q_ref, *refs):
    key_refs = refs[:key_count]
    refs = refs[key_count:]
    q = q_ref[...]
    if first:
        highest = weight_sum = acc = None
    else:
        stat_ref, acc_ref = refs[:2]
        refs = refs[2:]
        highest = stat_ref[:, 0:1]
        weight_sum = stat_ref[:, 128:129]
        acc = acc_ref[...]
    blocks = [
        (k_ref, at) for k_ref in key_refs for at in range(0, k_ref.shape[1], KEY_BLOCK)
    ]

    def scores_of(block):
        k_ref, at = block
        return jnp.dot(
            q, k_ref[:, at : at + KEY_BLOCK], preferred_element_type=jnp.float32
        )

    scores = scores_of(blocks[0])
    for place, (k_ref, at) in enumerate(blocks):
        upcoming = scores_of(blocks[place + 1]) if place + 1 < len(blocks) else None
        block_highest = jnp.max(scores, axis=1, keepdims=True)
        new_highest = (
            block_highest if highest is None else jnp.maximum(highest, block_highest)
        )
        w = jnp.exp2((scores - new_highest) * exponent_scale)
        part_sum = jnp.sum(w, axis=1, keepdims=True)
        part = lax.dot_general(
            w.astype(jnp.bfloat16),
            k_ref[:width, at : at + KEY_BLOCK],
            (((1,), (1,)), ((), ())),
            preferred_element_type=jnp.float32,
        )
        if highest is None:
            weight_sum, acc = part_sum, part
        else:
            fade = jnp.exp2((highest - new_highest) * exponent_scale)
            weight_sum = weight_sum * fade + part_sum
            acc = acc * fade + part
        highest, scores = new_highest, upcoming
    if last:
        (out_ref,) = refs
        out_ref[:, :width], out_ref[:, width:] = pack(acc, weight_sum, highest, exponent_scale)
    else:
        out_stat_ref, out_acc_ref = refs
        out_stat_ref[:, :128] = jnp.broadcast_to(highest, (q.shape[0], 128))
        out_stat_ref[:, 128:] = jnp.broadcast_to(weight_sum, (q.shape[0], 128))
        out_acc_ref[...] = acc


def attend(q, keys, state, last, width, exponent_scale, second=False, cost=COST):
    rows, features = q.shape
    first = state is None
    row_map = lambda i: (i, 0)
    all_map = lambda i: (0, 0)
    in_specs = [pl.BlockSpec((ROW_BLOCK, features), row_map)]
    in_specs += [pl.BlockSpec(k.shape, all_map) for k in keys]
    args = [q, *keys]
    state_specs = (
        pl.BlockSpec((ROW_BLOCK, 256), row_map),
        pl.BlockSpec((ROW_BLOCK, width), row_map),
    )
    skip = rows // ROW_BLOCK if second else 0
    old_map = lambda i: (i + skip, 0)
    if not first:
        in_specs += [
            pl.BlockSpec((ROW_BLOCK, 256), old_map),
            pl.BlockSpec((ROW_BLOCK, width), old_map),
        ]
        args += list(state)
    if last:
        out_shape = jax.ShapeDtypeStruct((rows, width + 128), jnp.bfloat16)
        out_specs = pl.BlockSpec((ROW_BLOCK, width + 128), row_map)
    else:
        out_shape = (
            jax.ShapeDtypeStruct((rows, 256), jnp.float32),
            jax.ShapeDtypeStruct((rows, width), jnp.float32),
        )
        out_specs = state_specs
    return pl.pallas_call(
        functools.partial(attend_kernel, first, last, width, exponent_scale, len(keys)),
        grid=(rows // ROW_BLOCK,),
        in_specs=in_specs,
        out_specs=out_specs,
        out_shape=out_shape,
        compiler_params=pltpu.CompilerParams(vmem_limit_bytes=VMEM),
        cost_estimate=cost,
        name="prefix_attend",
    )(*args)


def tail_kernel(span, width, exponent_scale, length_ref, joined_ref, out_ref):
    sources, _, tall, features = joined_ref.shape
    heads = tall - span
    keys = joined_ref[:, 0, :span].reshape(sources * span, features)
    q = joined_ref[:, 0, span:].reshape(sources * heads, features)
    s = lax.dot_general(q, keys, (((1,), (1,)), ((), ())), preferred_element_type=jnp.float32)
    usable = lax.broadcasted_iota(jnp.int32, s.shape, 1) < length_ref[pl.program_id(0)]
    s = jnp.where(usable, s, -1e30)
    highest = jnp.max(s, axis=1, keepdims=True)
    w = jnp.where(usable, jnp.exp2((s - highest) * exponent_scale), 0.0)
    weight_sum = jnp.sum(w, axis=1, keepdims=True)
    acc = jnp.dot(w.astype(jnp.bfloat16), keys[:, :width], preferred_element_type=jnp.float32)
    context, level = pack(acc, weight_sum, highest, exponent_scale)
    out_ref[:, 0, :, :width] = context.reshape(sources, heads, width)
    out_ref[:, 0, :, width:] = level.reshape(sources, heads, 128)


def attend_tails(joined, span, length, width, exponent_scale):
    sources, slots, tall, features = joined.shape
    heads = tall - span
    block = lambda last2, last1: pl.BlockSpec(
        (sources, 1, last2, last1), lambda i, *_: (0, i, 0, 0)
    )
    return pl.pallas_call(
        functools.partial(tail_kernel, span, width, exponent_scale),
        grid_spec=pltpu.PrefetchScalarGridSpec(
            num_scalar_prefetch=1,
            grid=(slots,),
            in_specs=[block(tall, features)],
            out_specs=block(heads, width + 128),
        ),
        out_shape=jax.ShapeDtypeStruct((sources, slots, heads, width + 128), jnp.bfloat16),
        compiler_params=pltpu.CompilerParams(vmem_limit_bytes=VMEM),
        cost_estimate=COST,
        name="tail_attend",
    )(length, joined)


def project(core, order_ref, head, proj_ref, keep_ref, give_ref, block_refs, sems, between):
    columns = block_refs.shape[2]
    copies = [
        pltpu.make_async_copy(
            proj_ref.at[:, pl.ds(pl.multiple_of(order_ref[i] * columns, 128), columns)],
            block_refs.at[i],
            sems.at[i],
        )
        for i in range(block_refs.shape[0])
    ]
    for copy in copies:
        copy.start()
    head = between() if head is None else head
    half = columns // 2
    early = core == 0
    for i, copy in enumerate(copies):
        copy.wait()
        mixed = jnp.dot(head, block_refs[i], preferred_element_type=jnp.float32)
        mixed = mixed.astype(jnp.bfloat16)
        keep_ref[i] = jnp.where(early, mixed[:, :half], mixed[:, half:])
        give_ref[i] = jnp.where(early, mixed[:, half:], mixed[:, :half])


def first_kernel(
    width, core_ref, order_ref, own_ref, received_ref, tail_ref, up_ref, proj_ref,
    keep_ref, give_ref, head_ref, context_ref, block_refs, sems,
):
    heads, _, value_width = up_ref.shape
    req_rows = head_ref.shape[0]

    def make_head():
        refs = (own_ref, received_ref, tail_ref)
        levels = [
            jnp.sum(ref[:, width:].astype(jnp.float32), axis=1, keepdims=True) for ref in refs
        ]
        top = functools.reduce(jnp.maximum, levels)
        shares = [jnp.exp2(level - top) for level in levels]
        total = shares[0] + shares[1] + shares[2]
        context = sum(
            ref[:, :width].astype(jnp.float32) * (share / total)
            for ref, share in zip(refs, shares)
        )
        context_ref[...] = context.reshape(req_rows, heads, width)
        for h in range(heads):
            head_ref[:, h * value_width : (h + 1) * value_width] = jnp.dot(
                context_ref[:, h, :].astype(jnp.bfloat16),
                up_ref[h],
                preferred_element_type=jnp.float32,
            ).astype(jnp.bfloat16)
        return head_ref[...]

    project(
        core_ref[0], order_ref, None, proj_ref, keep_ref, give_ref, block_refs, sems, make_head
    )


def second_kernel(
    core_ref, order_ref, head_ref, proj_ref, keep_ref, give_ref, block_refs, sems
):
    project(
        core_ref[0], order_ref, head_ref[...], proj_ref, keep_ref, give_ref, block_refs, sems, None
    )


def finish(args, head, out_proj, value_up, core, order, chips):
    heads, width, value_width = value_up.shape
    depth, columns = out_proj.shape
    block = columns // chips
    count = order.shape[0]
    vmem = pl.BlockSpec(memory_space=pltpu.VMEM)
    smem = pl.BlockSpec(memory_space=pltpu.SMEM)
    req_rows = (args[0].shape[0] // heads) if head is None else head.shape[0]
    half = jax.ShapeDtypeStruct((count, req_rows, block // 2), jnp.bfloat16)
    scratch = [
        pltpu.VMEM((count, depth, block), jnp.bfloat16),
        pltpu.SemaphoreType.DMA((count,)),
    ]
    common = dict(
        compiler_params=pltpu.CompilerParams(vmem_limit_bytes=VMEM), cost_estimate=COST
    )
    anywhere = pl.BlockSpec(memory_space=pl.ANY)
    if head is None:
        return pl.pallas_call(
            functools.partial(first_kernel, width),
            in_specs=[smem, smem, vmem, vmem, vmem, vmem, anywhere],
            out_specs=(vmem, vmem, vmem),
            out_shape=(
                half,
                half,
                jax.ShapeDtypeStruct((req_rows, heads * value_width), jnp.bfloat16),
            ),
            scratch_shapes=[pltpu.VMEM((req_rows, heads, width), jnp.float32)] + scratch,
            name="finish_first",
            **common,
        )(core, order, *args, value_up, out_proj)
    return pl.pallas_call(
        second_kernel,
        in_specs=[smem, smem, vmem, anywhere],
        out_specs=(vmem, vmem),
        out_shape=(half, half),
        scratch_shapes=scratch,
        name="finish_second",
        **common,
    )(core, order, head, out_proj)


def on_device(
    queries, prefix_latent, tail_latent, tail_length, slot_request, key_absorb, value_up, out_proj
):
    heads_here, nope_width, latent_width = key_absorb.shape
    value_width = value_up.shape[2]
    req_rows = slot_request.shape[0]
    features = prefix_latent.shape[1]
    rope_width = features - latent_width
    exponent_scale = math.log2(math.e) / math.sqrt(nope_width + rope_width)
    core = lax.axis_index("core")
    core_at = core.reshape(1)
    z_high, y_at = lax.axis_index("z_hi"), lax.axis_index("y")
    high_size, y_size = lax.axis_size("z_hi"), lax.axis_size("y")
    chips = high_size * y_size
    devices = chips * 2
    device = (z_high * y_size + y_at) * 2 + core
    slots = -(-req_rows // devices)
    span = tail_latent.shape[1]

    def ring(value, axis, by):
        size = lax.axis_size(axis)
        return lax.ppermute(value, axis, [(i, (i + by) % size) for i in range(size)])

    def other_core(value):
        return lax.ppermute(value, "core", [(0, 1), (1, 0)])

    def z_ring(value, by):
        low, high = lax.axis_size("z_lo"), lax.axis_size("z_hi")
        size = low * high
        place = lambda z: (z % low) * high + z // low
        pairs = [(place(z), place((z + by) % size)) for z in range(size)]
        return lax.ppermute(value, ("z_lo", "z_hi"), pairs)

    def exchange(value):
        return lax.all_to_all(value, ("z_hi", "y", "core"), 0, 0, tiled=True)

    def chip_shift(value, by_high, by_y):
        place = lambda z, y: (z % high_size) * y_size + y % y_size
        pairs = [
            (place(z, y), place(z + by_high, y + by_y))
            for z in range(high_size)
            for y in range(y_size)
        ]
        return lax.ppermute(value, ("z_hi", "y"), pairs)

    picked = jnp.take(queries, slot_request, axis=0).reshape(
        req_rows, heads_here, nope_width + rope_width
    )
    query_latent = jnp.einsum(
        "rhn,hnl->rhl", picked[:, :, :nope_width], key_absorb, preferred_element_type=jnp.float32
    ).astype(jnp.bfloat16)
    query_full = jnp.concatenate([query_latent, picked[:, :, nope_width:]], axis=2)
    query_rows = query_full.reshape(req_rows * heads_here, features)

    held = jnp.concatenate(
        [prefix_latent] + [ring(prefix_latent, "y", by) for by in (1, -1, 2)], axis=0
    ).T
    shifted = [z_ring(held, by) for by in (1, -1, 2)]
    held = [
        jnp.concatenate([held, shifted[0]], axis=1),
        jnp.concatenate([shifted[1], shifted[2]], axis=1),
    ]
    joined = jnp.pad(
        jnp.concatenate([tail_latent, query_full], axis=1),
        ((0, slots * devices - req_rows), (0, 0), (0, 0)),
    )
    query_other = other_core(query_rows)
    both = jnp.concatenate([query_rows, query_other], axis=0)
    both, held, joined = lax.optimization_barrier((both, held, joined))

    right = [ring(half, "x", 1) for half in held]
    left = [ring(half, "x", -1) for half in held]

    joined = exchange(joined).reshape(devices, slots, span + heads_here, features)
    length = lax.dynamic_slice_in_dim(
        jnp.pad(tail_length, (0, slots * devices - req_rows), constant_values=1),
        device * slots,
        slots,
    )

    go = functools.partial(attend, width=latent_width, exponent_scale=exponent_scale)
    far = [ring(right[0], "x", 1), ring(left[1], "x", -1)]
    state = go(both, held, None, False)

    state = go(both, right + left, state, False, cost=None)
    joined, state = lax.optimization_barrier((joined, state))
    tail_part = attend_tails(joined, span, length, latent_width, exponent_scale)
    tail_part, state = lax.optimization_barrier((tail_part, state))
    tail_part = exchange(tail_part.reshape(devices * slots, heads_here, latent_width + 128))
    tail_part = tail_part[:req_rows].reshape(req_rows * heads_here, latent_width + 128)

    packed_other = go(query_other, far, state, True, second=True, cost=None)
    received = other_core(packed_other)
    packed_own = go(query_rows, far, state, True, cost=None)

    moves = [(1, by) for by in range(y_size)] + [(0, by) for by in (1, 2, 3, 0)]
    order = jnp.stack(
        [
            ((z_high + by_high) % high_size) * y_size + (y_at + by_y) % y_size
            for by_high, by_y in moves
        ]
    ).astype(jnp.int32)
    run = functools.partial(
        finish, out_proj=out_proj, value_up=value_up, core=core_at, chips=chips
    )
    keep, give, head = run((packed_own, received, tail_part), None, order=order[:y_size])
    first = (keep, other_core(give))
    keep, give = run((), head, order=order[y_size:])
    second = (keep, other_core(give))
    paired = [
        (mine[i].astype(jnp.float32) + theirs[i].astype(jnp.float32))
        for mine, theirs in (first, second)
        for i in range(y_size)
    ]
    total = paired[-1]
    for (by_high, by_y), value in zip(moves[:-1], paired[:-1]):
        total += chip_shift(value.astype(jnp.bfloat16), by_high, by_y).astype(jnp.float32)
    return total.astype(jnp.bfloat16)


def solution(mesh):
    fine = Mesh(
        mesh.devices.reshape(4, 2, 2, 4, 2), ("x", "z_lo", "z_hi", "y", "core")
    )
    group, seq = ("x", "z_lo"), ("z_hi", "y", "core")
    placed = (
        P(None, seq),
        P(group + seq, None),
        P(group, seq, None),
        P(group),
        P(group),
        P(seq, None, None),
        P(seq, None, None),
        P(seq, None),
    )
    return jax.shard_map(
        on_device, mesh=fine, in_specs=placed, out_specs=P(group, seq), check_vma=False
    )
```

```python
import functools
import math

import jax
import jax.numpy as jnp
from jax import lax
from jax.experimental import pallas as pl
from jax.experimental.pallas import tpu as pltpu
from jax.sharding import Mesh, PartitionSpec as P

ROW_BLOCK = 288
KEY_BLOCK = 512
VMEM = 58 * 1024 * 1024
COST = None


def pack(acc, weight_sum, highest, exponent_scale):
    context = (acc / weight_sum).astype(jnp.bfloat16)
    level = highest * exponent_scale + jnp.log2(weight_sum)
    high = level.astype(jnp.bfloat16).astype(jnp.float32)
    middle = (level - high).astype(jnp.bfloat16).astype(jnp.float32)
    low = level - high - middle
    lane = lax.broadcasted_iota(jnp.int32, (acc.shape[0], 128), 1)
    terms = jnp.where(
        lane == 0, high, jnp.where(lane == 1, middle, jnp.where(lane == 2, low, 0.0))
    )
    return context, terms.astype(jnp.bfloat16)


def attend_kernel(first, last, width, exponent_scale, key_count, q_ref, *refs):
    key_refs = refs[:key_count]
    refs = refs[key_count:]
    q = q_ref[...]
    if first:
        highest = weight_sum = acc = None
    else:
        stat_ref, acc_ref = refs[:2]
        refs = refs[2:]
        highest = stat_ref[:, 0:1]
        weight_sum = stat_ref[:, 128:129]
        acc = acc_ref[...]
    blocks = [
        (k_ref, at) for k_ref in key_refs for at in range(0, k_ref.shape[1], KEY_BLOCK)
    ]

    def scores_of(block):
        k_ref, at = block
        return jnp.dot(
            q, k_ref[:, at : at + KEY_BLOCK], preferred_element_type=jnp.float32
        )

    scores = scores_of(blocks[0])
    for place, (k_ref, at) in enumerate(blocks):
        upcoming = scores_of(blocks[place + 1]) if place + 1 < len(blocks) else None
        block_highest = jnp.max(scores, axis=1, keepdims=True)
        new_highest = (
            block_highest if highest is None else jnp.maximum(highest, block_highest)
        )
        w = jnp.exp2((scores - new_highest) * exponent_scale)
        part_sum = jnp.sum(w, axis=1, keepdims=True)
        part = lax.dot_general(
            w.astype(jnp.bfloat16),
            k_ref[:width, at : at + KEY_BLOCK],
            (((1,), (1,)), ((), ())),
            preferred_element_type=jnp.float32,
        )
        if highest is None:
            weight_sum, acc = part_sum, part
        else:
            fade = jnp.exp2((highest - new_highest) * exponent_scale)
            weight_sum = weight_sum * fade + part_sum
            acc = acc * fade + part
        highest, scores = new_highest, upcoming
    if last:
        (out_ref,) = refs
        out_ref[:, :width], out_ref[:, width:] = pack(acc, weight_sum, highest, exponent_scale)
    else:
        out_stat_ref, out_acc_ref = refs
        out_stat_ref[:, :128] = jnp.broadcast_to(highest, (q.shape[0], 128))
        out_stat_ref[:, 128:] = jnp.broadcast_to(weight_sum, (q.shape[0], 128))
        out_acc_ref[...] = acc


def attend(q, keys, state, last, width, exponent_scale, second=False):
    rows, features = q.shape
    first = state is None
    row_map = lambda i: (i, 0)
    all_map = lambda i: (0, 0)
    in_specs = [pl.BlockSpec((ROW_BLOCK, features), row_map)]
    in_specs += [pl.BlockSpec(k.shape, all_map) for k in keys]
    args = [q, *keys]
    state_specs = (
        pl.BlockSpec((ROW_BLOCK, 256), row_map),
        pl.BlockSpec((ROW_BLOCK, width), row_map),
    )
    skip = rows // ROW_BLOCK if second else 0
    old_map = lambda i: (i + skip, 0)
    if not first:
        in_specs += [
            pl.BlockSpec((ROW_BLOCK, 256), old_map),
            pl.BlockSpec((ROW_BLOCK, width), old_map),
        ]
        args += list(state)
    if last:
        out_shape = jax.ShapeDtypeStruct((rows, width + 128), jnp.bfloat16)
        out_specs = pl.BlockSpec((ROW_BLOCK, width + 128), row_map)
    else:
        out_shape = (
            jax.ShapeDtypeStruct((rows, 256), jnp.float32),
            jax.ShapeDtypeStruct((rows, width), jnp.float32),
        )
        out_specs = state_specs
    return pl.pallas_call(
        functools.partial(attend_kernel, first, last, width, exponent_scale, len(keys)),
        grid=(rows // ROW_BLOCK,),
        in_specs=in_specs,
        out_specs=out_specs,
        out_shape=out_shape,
        compiler_params=pltpu.CompilerParams(vmem_limit_bytes=VMEM),
        cost_estimate=COST,
        name="prefix_attend",
    )(*args)


def tail_kernel(span, width, exponent_scale, length_ref, joined_ref, out_ref):
    sources, _, tall, features = joined_ref.shape
    heads = tall - span
    keys = joined_ref[:, 0, :span].reshape(sources * span, features)
    q = joined_ref[:, 0, span:].reshape(sources * heads, features)
    s = lax.dot_general(q, keys, (((1,), (1,)), ((), ())), preferred_element_type=jnp.float32)
    usable = lax.broadcasted_iota(jnp.int32, s.shape, 1) < length_ref[pl.program_id(0)]
    s = jnp.where(usable, s, -1e30)
    highest = jnp.max(s, axis=1, keepdims=True)
    w = jnp.where(usable, jnp.exp2((s - highest) * exponent_scale), 0.0)
    weight_sum = jnp.sum(w, axis=1, keepdims=True)
    acc = jnp.dot(w.astype(jnp.bfloat16), keys[:, :width], preferred_element_type=jnp.float32)
    context, level = pack(acc, weight_sum, highest, exponent_scale)
    out_ref[:, 0, :, :width] = context.reshape(sources, heads, width)
    out_ref[:, 0, :, width:] = level.reshape(sources, heads, 128)


def attend_tails(joined, span, length, width, exponent_scale):
    sources, slots, tall, features = joined.shape
    heads = tall - span
    block = lambda last2, last1: pl.BlockSpec(
        (sources, 1, last2, last1), lambda i, *_: (0, i, 0, 0)
    )
    return pl.pallas_call(
        functools.partial(tail_kernel, span, width, exponent_scale),
        grid_spec=pltpu.PrefetchScalarGridSpec(
            num_scalar_prefetch=1,
            grid=(slots,),
            in_specs=[block(tall, features)],
            out_specs=block(heads, width + 128),
        ),
        out_shape=jax.ShapeDtypeStruct((sources, slots, heads, width + 128), jnp.bfloat16),
        compiler_params=pltpu.CompilerParams(vmem_limit_bytes=VMEM),
        cost_estimate=COST,
        name="tail_attend",
    )(length, joined)


def finish_kernel(
    width, core_ref, order_ref, own_ref, received_ref, tail_ref, up_ref, proj_ref,
    keep_ref, give_ref, head_ref, context_ref, block_refs, sems,
):
    columns = block_refs.shape[2]
    copies = [
        pltpu.make_async_copy(
            proj_ref.at[:, pl.ds(pl.multiple_of(order_ref[i] * columns, 128), columns)],
            block_refs.at[i],
            sems.at[i],
        )
        for i in range(block_refs.shape[0])
    ]
    for copy in copies:
        copy.start()
    heads, _, value_width = up_ref.shape
    req_rows = head_ref.shape[0]
    refs = (own_ref, received_ref, tail_ref)
    levels = [
        jnp.sum(ref[:, width:].astype(jnp.float32), axis=1, keepdims=True) for ref in refs
    ]
    top = functools.reduce(jnp.maximum, levels)
    shares = [jnp.exp2(level - top) for level in levels]
    total = shares[0] + shares[1] + shares[2]
    context = sum(
        ref[:, :width].astype(jnp.float32) * (share / total)
        for ref, share in zip(refs, shares)
    )
    context_ref[...] = context.reshape(req_rows, heads, width)
    for h in range(heads):
        head_ref[:, h * value_width : (h + 1) * value_width] = jnp.dot(
            context_ref[:, h, :].astype(jnp.bfloat16),
            up_ref[h],
            preferred_element_type=jnp.float32,
        ).astype(jnp.bfloat16)
    head = head_ref[...]
    half = keep_ref.shape[2]
    early = core_ref[0] == 0
    for i, copy in enumerate(copies):
        copy.wait()
        mixed = jnp.dot(head, block_refs[i], preferred_element_type=jnp.float32)
        mixed = mixed.astype(jnp.bfloat16)
        keep_ref[i] = jnp.where(early, mixed[:, :half], mixed[:, half:])
        give_ref[i] = jnp.where(early, mixed[:, half:], mixed[:, :half])


def finish(own, received, tail, value_up, out_proj, core, order):
    heads, width, value_width = value_up.shape
    req_rows = own.shape[0] // heads
    vmem = pl.BlockSpec(memory_space=pltpu.VMEM)
    smem = pl.BlockSpec(memory_space=pltpu.SMEM)
    chips = order.shape[0]
    half = jax.ShapeDtypeStruct((chips, req_rows, out_proj.shape[1] // (2 * chips)), jnp.bfloat16)
    return pl.pallas_call(
        functools.partial(finish_kernel, width),
        in_specs=[smem, smem, vmem, vmem, vmem, vmem, pl.BlockSpec(memory_space=pl.ANY)],
        out_specs=(vmem, vmem),
        out_shape=(half, half),
        scratch_shapes=[
            pltpu.VMEM((req_rows, heads * value_width), jnp.bfloat16),
            pltpu.VMEM((req_rows, heads, width), jnp.float32),
            pltpu.VMEM((chips, out_proj.shape[0], out_proj.shape[1] // chips), jnp.bfloat16),
            pltpu.SemaphoreType.DMA((chips,)),
        ],
        compiler_params=pltpu.CompilerParams(vmem_limit_bytes=VMEM),
        cost_estimate=COST,
        name="finish",
    )(core, order, own, received, tail, value_up, out_proj)


def on_device(
    queries, prefix_latent, tail_latent, tail_length, slot_request, key_absorb, value_up, out_proj
):
    heads_here, nope_width, latent_width = key_absorb.shape
    value_width = value_up.shape[2]
    req_rows = slot_request.shape[0]
    features = prefix_latent.shape[1]
    rope_width = features - latent_width
    exponent_scale = math.log2(math.e) / math.sqrt(nope_width + rope_width)
    core = lax.axis_index("core")
    core_at = core.reshape(1)
    z_high, y_at = lax.axis_index("z_hi"), lax.axis_index("y")
    high_size, y_size = lax.axis_size("z_hi"), lax.axis_size("y")
    chips = high_size * y_size
    devices = chips * 2
    device = (z_high * y_size + y_at) * 2 + core
    slots = -(-req_rows // devices)
    span = tail_latent.shape[1]

    def ring(value, axis, by):
        size = lax.axis_size(axis)
        return lax.ppermute(value, axis, [(i, (i + by) % size) for i in range(size)])

    def other_core(value):
        return lax.ppermute(value, "core", [(0, 1), (1, 0)])

    def z_ring(value, by):
        low, high = lax.axis_size("z_lo"), lax.axis_size("z_hi")
        size = low * high
        place = lambda z: (z % low) * high + z // low
        pairs = [(place(z), place((z + by) % size)) for z in range(size)]
        return lax.ppermute(value, ("z_lo", "z_hi"), pairs)

    def exchange(value):
        return lax.all_to_all(value, ("z_hi", "y", "core"), 0, 0, tiled=True)

    def chip_shift(value, by_high, by_y):
        place = lambda z, y: (z % high_size) * y_size + y % y_size
        pairs = [
            (place(z, y), place(z + by_high, y + by_y))
            for z in range(high_size)
            for y in range(y_size)
        ]
        return lax.ppermute(value, ("z_hi", "y"), pairs)

    picked = jnp.take(queries, slot_request, axis=0).reshape(
        req_rows, heads_here, nope_width + rope_width
    )
    query_latent = jnp.einsum(
        "rhn,hnl->rhl", picked[:, :, :nope_width], key_absorb, preferred_element_type=jnp.float32
    ).astype(jnp.bfloat16)
    query_full = jnp.concatenate([query_latent, picked[:, :, nope_width:]], axis=2)
    query_rows = query_full.reshape(req_rows * heads_here, features)

    held = jnp.concatenate(
        [prefix_latent] + [ring(prefix_latent, "y", by) for by in (1, -1, 2)], axis=0
    ).T
    shifted = [z_ring(held, by) for by in (1, -1, 2)]
    held = [
        jnp.concatenate([held, shifted[0]], axis=1),
        jnp.concatenate([shifted[1], shifted[2]], axis=1),
    ]
    joined = jnp.pad(
        jnp.concatenate([tail_latent, query_full], axis=1),
        ((0, slots * devices - req_rows), (0, 0), (0, 0)),
    )
    query_other = other_core(query_rows)
    both = jnp.concatenate([query_rows, query_other], axis=0)
    both, held, joined = lax.optimization_barrier((both, held, joined))

    right = [ring(half, "x", 1) for half in held]
    left = [ring(half, "x", -1) for half in held]

    joined = exchange(joined).reshape(devices, slots, span + heads_here, features)
    length = lax.dynamic_slice_in_dim(
        jnp.pad(tail_length, (0, slots * devices - req_rows), constant_values=1),
        device * slots,
        slots,
    )

    go = functools.partial(attend, width=latent_width, exponent_scale=exponent_scale)
    state = go(both, held, None, False)
    near = [right[0], left[1]]
    near, state = lax.optimization_barrier((near, state))
    far = [ring(near[0], "x", 1), ring(near[1], "x", -1)]

    state = go(both, near, state, False)
    joined, state = lax.optimization_barrier((joined, state))
    tail_part = attend_tails(joined, span, length, latent_width, exponent_scale)
    tail_part, state = lax.optimization_barrier((tail_part, state))
    late = [right[1], left[0]] + far
    tail_part = exchange(tail_part.reshape(devices * slots, heads_here, latent_width + 128))
    tail_part = tail_part[:req_rows].reshape(req_rows * heads_here, latent_width + 128)

    packed_other = go(query_other, late, state, True, second=True)
    received = other_core(packed_other)
    packed_own = go(query_rows, late, state, True)

    moves = [(by_y, by_high) for by_y in (1, 2, 3, 0) for by_high in range(high_size)]
    order = jnp.stack(
        [
            ((z_high + by_high) % high_size) * y_size + (y_at + by_y) % y_size
            for by_y, by_high in moves
        ]
    ).astype(jnp.int32)
    keep, give = finish(packed_own, received, tail_part, value_up, out_proj, core_at, order)
    given = other_core(give)
    sums = [
        (keep[at : at + high_size].astype(jnp.float32) + given[at : at + high_size].astype(jnp.float32))
        for at in range(0, chips, high_size)
    ]
    total = sums[-1]
    for by_y, value in zip((1, 2, 3), sums[:-1]):
        total += ring(value.astype(jnp.bfloat16), "y", by_y).astype(jnp.float32)
    passed = ring(total[1].astype(jnp.bfloat16), "z_hi", 1)
    return (total[0] + passed.astype(jnp.float32)).astype(jnp.bfloat16)


def solution(mesh):
    fine = Mesh(
        mesh.devices.reshape(4, 2, 2, 4, 2), ("x", "z_lo", "z_hi", "y", "core")
    )
    group, seq = ("x", "z_lo"), ("z_hi", "y", "core")
    placed = (
        P(None, seq),
        P(group + seq, None),
        P(group, seq, None),
        P(group),
        P(group),
        P(seq, None, None),
        P(seq, None, None),
        P(seq, None),
    )
    return jax.shard_map(
        on_device, mesh=fine, in_specs=placed, out_specs=P(group, seq), check_vma=False
    )
```

```python
import functools
import math

import jax
import jax.numpy as jnp
from jax import lax
from jax.experimental import pallas as pl
from jax.experimental.pallas import tpu as pltpu
from jax.sharding import Mesh, PartitionSpec as P

ROW_BLOCK = 288
KEY_BLOCK = 512
VMEM = 58 * 1024 * 1024
COST = None


def pack(acc, weight_sum, highest, exponent_scale):
    context = (acc / weight_sum).astype(jnp.bfloat16)
    level = highest * exponent_scale + jnp.log2(weight_sum)
    high = level.astype(jnp.bfloat16).astype(jnp.float32)
    middle = (level - high).astype(jnp.bfloat16).astype(jnp.float32)
    low = level - high - middle
    lane = lax.broadcasted_iota(jnp.int32, (acc.shape[0], 128), 1)
    terms = jnp.where(
        lane == 0, high, jnp.where(lane == 1, middle, jnp.where(lane == 2, low, 0.0))
    )
    return context, terms.astype(jnp.bfloat16)


def attend_kernel(first, last, width, exponent_scale, key_count, q_ref, *refs):
    key_refs = refs[:key_count]
    refs = refs[key_count:]
    q = q_ref[...]
    if first:
        highest = weight_sum = acc = None
    else:
        stat_ref, acc_ref = refs[:2]
        refs = refs[2:]
        highest = stat_ref[:, 0:1]
        weight_sum = stat_ref[:, 128:129]
        acc = acc_ref[...]
    blocks = [
        (k_ref, at) for k_ref in key_refs for at in range(0, k_ref.shape[1], KEY_BLOCK)
    ]

    def scores_of(block):
        k_ref, at = block
        return jnp.dot(
            q, k_ref[:, at : at + KEY_BLOCK], preferred_element_type=jnp.float32
        )

    scores = scores_of(blocks[0])
    for place, (k_ref, at) in enumerate(blocks):
        upcoming = scores_of(blocks[place + 1]) if place + 1 < len(blocks) else None
        block_highest = jnp.max(scores, axis=1, keepdims=True)
        new_highest = (
            block_highest if highest is None else jnp.maximum(highest, block_highest)
        )
        w = jnp.exp2((scores - new_highest) * exponent_scale)
        part_sum = jnp.sum(w, axis=1, keepdims=True)
        part = lax.dot_general(
            w.astype(jnp.bfloat16),
            k_ref[:width, at : at + KEY_BLOCK],
            (((1,), (1,)), ((), ())),
            preferred_element_type=jnp.float32,
        )
        if highest is None:
            weight_sum, acc = part_sum, part
        else:
            fade = jnp.exp2((highest - new_highest) * exponent_scale)
            weight_sum = weight_sum * fade + part_sum
            acc = acc * fade + part
        highest, scores = new_highest, upcoming
    if last:
        (out_ref,) = refs
        out_ref[:, :width], out_ref[:, width:] = pack(acc, weight_sum, highest, exponent_scale)
    else:
        out_stat_ref, out_acc_ref = refs
        out_stat_ref[:, :128] = jnp.broadcast_to(highest, (q.shape[0], 128))
        out_stat_ref[:, 128:] = jnp.broadcast_to(weight_sum, (q.shape[0], 128))
        out_acc_ref[...] = acc


def attend(q, keys, state, last, width, exponent_scale, second=False):
    rows, features = q.shape
    first = state is None
    row_map = lambda i: (i, 0)
    all_map = lambda i: (0, 0)
    in_specs = [pl.BlockSpec((ROW_BLOCK, features), row_map)]
    in_specs += [pl.BlockSpec(k.shape, all_map) for k in keys]
    args = [q, *keys]
    state_specs = (
        pl.BlockSpec((ROW_BLOCK, 256), row_map),
        pl.BlockSpec((ROW_BLOCK, width), row_map),
    )
    skip = rows // ROW_BLOCK if second else 0
    old_map = lambda i: (i + skip, 0)
    if not first:
        in_specs += [
            pl.BlockSpec((ROW_BLOCK, 256), old_map),
            pl.BlockSpec((ROW_BLOCK, width), old_map),
        ]
        args += list(state)
    if last:
        out_shape = jax.ShapeDtypeStruct((rows, width + 128), jnp.bfloat16)
        out_specs = pl.BlockSpec((ROW_BLOCK, width + 128), row_map)
    else:
        out_shape = (
            jax.ShapeDtypeStruct((rows, 256), jnp.float32),
            jax.ShapeDtypeStruct((rows, width), jnp.float32),
        )
        out_specs = state_specs
    return pl.pallas_call(
        functools.partial(attend_kernel, first, last, width, exponent_scale, len(keys)),
        grid=(rows // ROW_BLOCK,),
        in_specs=in_specs,
        out_specs=out_specs,
        out_shape=out_shape,
        compiler_params=pltpu.CompilerParams(vmem_limit_bytes=VMEM),
        cost_estimate=COST,
        name="prefix_attend",
    )(*args)


def tail_kernel(span, width, exponent_scale, length_ref, joined_ref, out_ref):
    sources, _, tall, features = joined_ref.shape
    heads = tall - span
    keys = joined_ref[:, 0, :span].reshape(sources * span, features)
    q = joined_ref[:, 0, span:].reshape(sources * heads, features)
    s = lax.dot_general(q, keys, (((1,), (1,)), ((), ())), preferred_element_type=jnp.float32)
    usable = lax.broadcasted_iota(jnp.int32, s.shape, 1) < length_ref[pl.program_id(0)]
    s = jnp.where(usable, s, -1e30)
    highest = jnp.max(s, axis=1, keepdims=True)
    w = jnp.where(usable, jnp.exp2((s - highest) * exponent_scale), 0.0)
    weight_sum = jnp.sum(w, axis=1, keepdims=True)
    acc = jnp.dot(w.astype(jnp.bfloat16), keys[:, :width], preferred_element_type=jnp.float32)
    context, level = pack(acc, weight_sum, highest, exponent_scale)
    out_ref[:, 0, :, :width] = context.reshape(sources, heads, width)
    out_ref[:, 0, :, width:] = level.reshape(sources, heads, 128)


def attend_tails(joined, span, length, width, exponent_scale):
    sources, slots, tall, features = joined.shape
    heads = tall - span
    block = lambda last2, last1: pl.BlockSpec(
        (sources, 1, last2, last1), lambda i, *_: (0, i, 0, 0)
    )
    return pl.pallas_call(
        functools.partial(tail_kernel, span, width, exponent_scale),
        grid_spec=pltpu.PrefetchScalarGridSpec(
            num_scalar_prefetch=1,
            grid=(slots,),
            in_specs=[block(tall, features)],
            out_specs=block(heads, width + 128),
        ),
        out_shape=jax.ShapeDtypeStruct((sources, slots, heads, width + 128), jnp.bfloat16),
        compiler_params=pltpu.CompilerParams(vmem_limit_bytes=VMEM),
        cost_estimate=COST,
        name="tail_attend",
    )(length, joined)


def finish_kernel(
    width, core_ref, order_ref, own_ref, received_ref, tail_ref, up_ref, proj_ref,
    keep_ref, give_ref, head_ref, context_ref, block_refs, sems,
):
    columns = block_refs.shape[2]
    copies = [
        pltpu.make_async_copy(
            proj_ref.at[:, pl.ds(pl.multiple_of(order_ref[i] * columns, 128), columns)],
            block_refs.at[i],
            sems.at[i],
        )
        for i in range(block_refs.shape[0])
    ]
    for copy in copies:
        copy.start()
    heads, _, value_width = up_ref.shape
    req_rows = head_ref.shape[0]
    refs = (own_ref, received_ref, tail_ref)
    rows = own_ref.shape[0]
    levels = [
        jnp.sum(ref[:rows, width:].astype(jnp.float32), axis=1, keepdims=True) for ref in refs
    ]
    top = functools.reduce(jnp.maximum, levels)
    shares = [jnp.exp2(level - top) for level in levels]
    total = shares[0] + shares[1] + shares[2]
    context = sum(
        ref[:rows, :width].astype(jnp.float32) * (share / total)
        for ref, share in zip(refs, shares)
    )
    context_ref[...] = context.reshape(req_rows, heads, width)
    for h in range(heads):
        head_ref[:, h * value_width : (h + 1) * value_width] = jnp.dot(
            context_ref[:, h, :].astype(jnp.bfloat16),
            up_ref[h],
            preferred_element_type=jnp.float32,
        ).astype(jnp.bfloat16)
    head = head_ref[...]
    half = keep_ref.shape[2]
    early = core_ref[0] == 0
    for i, copy in enumerate(copies):
        copy.wait()
        mixed = jnp.dot(head, block_refs[i], preferred_element_type=jnp.float32)
        mixed = mixed.astype(jnp.bfloat16)
        keep_ref[i] = jnp.where(early, mixed[:, :half], mixed[:, half:])
        give_ref[i] = jnp.where(early, mixed[:, half:], mixed[:, :half])


def finish(own, received, tail, value_up, out_proj, core, order):
    heads, width, value_width = value_up.shape
    req_rows = own.shape[0] // heads
    vmem = pl.BlockSpec(memory_space=pltpu.VMEM)
    smem = pl.BlockSpec(memory_space=pltpu.SMEM)
    chips = order.shape[0]
    half = jax.ShapeDtypeStruct((chips, req_rows, out_proj.shape[1] // (2 * chips)), jnp.bfloat16)
    return pl.pallas_call(
        functools.partial(finish_kernel, width),
        in_specs=[smem, smem, vmem, vmem, vmem, vmem, pl.BlockSpec(memory_space=pl.ANY)],
        out_specs=(vmem, vmem),
        out_shape=(half, half),
        scratch_shapes=[
            pltpu.VMEM((req_rows, heads * value_width), jnp.bfloat16),
            pltpu.VMEM((req_rows, heads, width), jnp.float32),
            pltpu.VMEM((chips, out_proj.shape[0], out_proj.shape[1] // chips), jnp.bfloat16),
            pltpu.SemaphoreType.DMA((chips,)),
        ],
        compiler_params=pltpu.CompilerParams(vmem_limit_bytes=VMEM),
        cost_estimate=COST,
        name="finish",
    )(core, order, own, received, tail, value_up, out_proj)


def on_device(
    queries, prefix_latent, tail_latent, tail_length, slot_request, key_absorb, value_up, out_proj
):
    heads_here, nope_width, latent_width = key_absorb.shape
    value_width = value_up.shape[2]
    req_rows = slot_request.shape[0]
    features = prefix_latent.shape[1]
    rope_width = features - latent_width
    exponent_scale = math.log2(math.e) / math.sqrt(nope_width + rope_width)
    core = lax.axis_index("core")
    core_at = core.reshape(1)
    z_high, y_at = lax.axis_index("z_hi"), lax.axis_index("y")
    high_size, y_size = lax.axis_size("z_hi"), lax.axis_size("y")
    chips = high_size * y_size
    devices = chips * 2
    device = (z_high * y_size + y_at) * 2 + core
    slots = -(-req_rows // devices)
    span = tail_latent.shape[1]

    def ring(value, axis, by):
        size = lax.axis_size(axis)
        return lax.ppermute(value, axis, [(i, (i + by) % size) for i in range(size)])

    def other_core(value):
        return lax.ppermute(value, "core", [(0, 1), (1, 0)])

    def z_ring(value, by):
        low, high = lax.axis_size("z_lo"), lax.axis_size("z_hi")
        size = low * high
        place = lambda z: (z % low) * high + z // low
        pairs = [(place(z), place((z + by) % size)) for z in range(size)]
        return lax.ppermute(value, ("z_lo", "z_hi"), pairs)

    def exchange(value):
        return lax.all_to_all(value, ("z_hi", "y", "core"), 0, 0, tiled=True)

    def chip_shift(value, by_high, by_y):
        place = lambda z, y: (z % high_size) * y_size + y % y_size
        pairs = [
            (place(z, y), place(z + by_high, y + by_y))
            for z in range(high_size)
            for y in range(y_size)
        ]
        return lax.ppermute(value, ("z_hi", "y"), pairs)

    picked = jnp.take(queries, slot_request, axis=0).reshape(
        req_rows, heads_here, nope_width + rope_width
    )
    query_latent = jnp.einsum(
        "rhn,hnl->rhl", picked[:, :, :nope_width], key_absorb, preferred_element_type=jnp.float32
    ).astype(jnp.bfloat16)
    query_full = jnp.concatenate([query_latent, picked[:, :, nope_width:]], axis=2)
    query_rows = query_full.reshape(req_rows * heads_here, features)

    columns = ("z_lo", "z_hi", "y")
    copies = math.prod(lax.axis_size(name) for name in columns)
    held = lax.all_to_all(
        jnp.broadcast_to(prefix_latent[None], (copies, *prefix_latent.shape)), columns, 0, 0
    )
    joined = jnp.pad(
        jnp.concatenate([tail_latent, query_full], axis=1),
        ((0, slots * devices - req_rows), (0, 0), (0, 0)),
    )
    query_rows, joined = lax.optimization_barrier((query_rows, joined))
    query_other = other_core(query_rows)
    both = jnp.concatenate([query_rows, query_other], axis=0)
    both, held, joined = lax.optimization_barrier((both, held, joined))
    held = held.reshape(2, -1, features)
    held = [held[0].T, held[1].T]

    right = [ring(half, "x", 1) for half in held]
    left = [ring(half, "x", -1) for half in held]

    joined = exchange(joined).reshape(devices, slots, span + heads_here, features)
    length = lax.dynamic_slice_in_dim(
        jnp.pad(tail_length, (0, slots * devices - req_rows), constant_values=1),
        device * slots,
        slots,
    )

    go = functools.partial(attend, width=latent_width, exponent_scale=exponent_scale)
    state = go(both, held, None, False)
    near = [right[0], left[1]]
    near, state = lax.optimization_barrier((near, state))
    far = [ring(near[0], "x", 1), ring(near[1], "x", -1)]

    state = go(both, near, state, False)
    joined, state = lax.optimization_barrier((joined, state))
    tail_part = attend_tails(joined, span, length, latent_width, exponent_scale)
    tail_part, state = lax.optimization_barrier((tail_part, state))
    late = [right[1], left[0]] + far
    tail_part = exchange(tail_part.reshape(devices * slots, heads_here, latent_width + 128))
    tail_part = tail_part.reshape(devices * slots * heads_here, latent_width + 128)

    packed_other = go(query_other, late, state, True, second=True)
    received = other_core(packed_other)
    packed_own = go(query_rows, late, state, True)

    moves = [(by_y, by_high) for by_y in (1, 2, 3, 0) for by_high in range(high_size)]
    order = jnp.stack(
        [
            ((z_high + by_high) % high_size) * y_size + (y_at + by_y) % y_size
            for by_y, by_high in moves
        ]
    ).astype(jnp.int32)
    keep, give = finish(packed_own, received, tail_part, value_up, out_proj, core_at, order)
    given = other_core(give)
    sums = [
        (keep[at : at + high_size].astype(jnp.float32) + given[at : at + high_size].astype(jnp.float32))
        for at in range(0, chips, high_size)
    ]
    total = sums[-1]
    for by_y, value in zip((1, 2, 3), sums[:-1]):
        total += ring(value.astype(jnp.bfloat16), "y", by_y).astype(jnp.float32)
    passed = ring(total[1].astype(jnp.bfloat16), "z_hi", 1)
    return (total[0] + passed.astype(jnp.float32)).astype(jnp.bfloat16)


def solution(mesh):
    fine = Mesh(
        mesh.devices.reshape(4, 2, 2, 4, 2), ("x", "z_lo", "z_hi", "y", "core")
    )
    group, seq = ("x", "z_lo"), ("z_hi", "y", "core")
    placed = (
        P(None, seq),
        P(group + seq, None),
        P(group, seq, None),
        P(group),
        P(group),
        P(seq, None, None),
        P(seq, None, None),
        P(seq, None),
    )
    return jax.shard_map(
        on_device, mesh=fine, in_specs=placed, out_specs=P(group, seq), check_vma=False
    )
```

```python
import functools
import math

import jax
import jax.numpy as jnp
from jax import lax
from jax.experimental import pallas as pl
from jax.experimental.pallas import tpu as pltpu
from jax.sharding import Mesh, PartitionSpec as P

ROW_BLOCK = 288
KEY_BLOCK = 512
VMEM = 58 * 1024 * 1024
COST = None


def pack(acc, weight_sum, highest, exponent_scale):
    context = (acc / weight_sum).astype(jnp.bfloat16)
    level = highest * exponent_scale + jnp.log2(weight_sum)
    high = level.astype(jnp.bfloat16).astype(jnp.float32)
    middle = (level - high).astype(jnp.bfloat16).astype(jnp.float32)
    low = level - high - middle
    lane = lax.broadcasted_iota(jnp.int32, (acc.shape[0], 128), 1)
    terms = jnp.where(
        lane == 0, high, jnp.where(lane == 1, middle, jnp.where(lane == 2, low, 0.0))
    )
    return context, terms.astype(jnp.bfloat16)


def attend_kernel(first, last, width, exponent_scale, key_count, q_ref, *refs):
    key_refs = refs[:key_count]
    refs = refs[key_count:]
    q = q_ref[...]
    if first:
        highest = weight_sum = acc = None
    else:
        stat_ref, acc_ref = refs[:2]
        refs = refs[2:]
        highest = stat_ref[:, 0:1]
        weight_sum = stat_ref[:, 128:129]
        acc = acc_ref[...]
    blocks = [
        (k_ref, at) for k_ref in key_refs for at in range(0, k_ref.shape[1], KEY_BLOCK)
    ]

    def scores_of(block):
        k_ref, at = block
        return jnp.dot(
            q, k_ref[:, at : at + KEY_BLOCK], preferred_element_type=jnp.float32
        )

    scores = scores_of(blocks[0])
    for place, (k_ref, at) in enumerate(blocks):
        upcoming = scores_of(blocks[place + 1]) if place + 1 < len(blocks) else None
        block_highest = jnp.max(scores, axis=1, keepdims=True)
        new_highest = (
            block_highest if highest is None else jnp.maximum(highest, block_highest)
        )
        w = jnp.exp2((scores - new_highest) * exponent_scale)
        part_sum = jnp.sum(w, axis=1, keepdims=True)
        part = lax.dot_general(
            w.astype(jnp.bfloat16),
            k_ref[:width, at : at + KEY_BLOCK],
            (((1,), (1,)), ((), ())),
            preferred_element_type=jnp.float32,
        )
        if highest is None:
            weight_sum, acc = part_sum, part
        else:
            fade = jnp.exp2((highest - new_highest) * exponent_scale)
            weight_sum = weight_sum * fade + part_sum
            acc = acc * fade + part
        highest, scores = new_highest, upcoming
    if last:
        (out_ref,) = refs
        out_ref[:, :width], out_ref[:, width:] = pack(acc, weight_sum, highest, exponent_scale)
    else:
        out_stat_ref, out_acc_ref = refs
        out_stat_ref[:, :128] = jnp.broadcast_to(highest, (q.shape[0], 128))
        out_stat_ref[:, 128:] = jnp.broadcast_to(weight_sum, (q.shape[0], 128))
        out_acc_ref[...] = acc


def attend(q, keys, state, last, width, exponent_scale, second=False):
    rows, features = q.shape
    first = state is None
    row_map = lambda i: (i, 0)
    all_map = lambda i: (0, 0)
    in_specs = [pl.BlockSpec((ROW_BLOCK, features), row_map)]
    in_specs += [pl.BlockSpec(k.shape, all_map) for k in keys]
    args = [q, *keys]
    state_specs = (
        pl.BlockSpec((ROW_BLOCK, 256), row_map),
        pl.BlockSpec((ROW_BLOCK, width), row_map),
    )
    skip = rows // ROW_BLOCK if second else 0
    old_map = lambda i: (i + skip, 0)
    if not first:
        in_specs += [
            pl.BlockSpec((ROW_BLOCK, 256), old_map),
            pl.BlockSpec((ROW_BLOCK, width), old_map),
        ]
        args += list(state)
    if last:
        out_shape = jax.ShapeDtypeStruct((rows, width + 128), jnp.bfloat16)
        out_specs = pl.BlockSpec((ROW_BLOCK, width + 128), row_map)
    else:
        out_shape = (
            jax.ShapeDtypeStruct((rows, 256), jnp.float32),
            jax.ShapeDtypeStruct((rows, width), jnp.float32),
        )
        out_specs = state_specs
    return pl.pallas_call(
        functools.partial(attend_kernel, first, last, width, exponent_scale, len(keys)),
        grid=(rows // ROW_BLOCK,),
        in_specs=in_specs,
        out_specs=out_specs,
        out_shape=out_shape,
        compiler_params=pltpu.CompilerParams(vmem_limit_bytes=VMEM),
        cost_estimate=COST,
        name="prefix_attend",
    )(*args)


def tail_kernel(span, width, exponent_scale, length_ref, joined_ref, out_ref):
    sources, slots, tall, features = joined_ref.shape
    heads = tall - span
    for slot in range(slots):
        keys = joined_ref[:, slot, :span].reshape(sources * span, features)
        q = joined_ref[:, slot, span:].reshape(sources * heads, features)
        s = lax.dot_general(q, keys, (((1,), (1,)), ((), ())), preferred_element_type=jnp.float32)
        usable = lax.broadcasted_iota(jnp.int32, s.shape, 1) < length_ref[slot]
        s = jnp.where(usable, s, -1e30)
        highest = jnp.max(s, axis=1, keepdims=True)
        w = jnp.where(usable, jnp.exp2((s - highest) * exponent_scale), 0.0)
        weight_sum = jnp.sum(w, axis=1, keepdims=True)
        acc = jnp.dot(w.astype(jnp.bfloat16), keys[:, :width], preferred_element_type=jnp.float32)
        context, level = pack(acc, weight_sum, highest, exponent_scale)
        out_ref[:, slot, :, :width] = context.reshape(sources, heads, width)
        out_ref[:, slot, :, width:] = level.reshape(sources, heads, 128)


def attend_tails(joined, span, length, width, exponent_scale):
    sources, slots, tall, features = joined.shape
    heads = tall - span
    block = lambda last2, last1: pl.BlockSpec(
        (sources, slots, last2, last1), lambda i, *_: (0, 0, 0, 0)
    )
    return pl.pallas_call(
        functools.partial(tail_kernel, span, width, exponent_scale),
        grid_spec=pltpu.PrefetchScalarGridSpec(
            num_scalar_prefetch=1,
            grid=(1,),
            in_specs=[block(tall, features)],
            out_specs=block(heads, width + 128),
        ),
        out_shape=jax.ShapeDtypeStruct((sources, slots, heads, width + 128), jnp.bfloat16),
        compiler_params=pltpu.CompilerParams(vmem_limit_bytes=VMEM),
        cost_estimate=COST,
        name="tail_attend",
    )(length, joined)


def finish_kernel(
    width, core_ref, order_ref, own_ref, received_ref, tail_ref, up_ref, proj_ref,
    keep_ref, give_ref, head_ref, context_ref, block_refs, sems,
):
    columns = block_refs.shape[2]
    copies = [
        pltpu.make_async_copy(
            proj_ref.at[:, pl.ds(pl.multiple_of(order_ref[i] * columns, 128), columns)],
            block_refs.at[i],
            sems.at[i],
        )
        for i in range(block_refs.shape[0])
    ]
    for copy in copies:
        copy.start()
    heads, _, value_width = up_ref.shape
    req_rows = head_ref.shape[0]
    refs = (own_ref, received_ref, tail_ref)
    rows = own_ref.shape[0]
    levels = [
        jnp.sum(ref[:rows, width:].astype(jnp.float32), axis=1, keepdims=True) for ref in refs
    ]
    top = functools.reduce(jnp.maximum, levels)
    shares = [jnp.exp2(level - top) for level in levels]
    total = shares[0] + shares[1] + shares[2]
    context = sum(
        ref[:rows, :width].astype(jnp.float32) * (share / total)
        for ref, share in zip(refs, shares)
    )
    context_ref[...] = context.reshape(req_rows, heads, width)
    for h in range(heads):
        head_ref[:, h * value_width : (h + 1) * value_width] = jnp.dot(
            context_ref[:, h, :].astype(jnp.bfloat16),
            up_ref[h],
            preferred_element_type=jnp.float32,
        ).astype(jnp.bfloat16)
    head = head_ref[...]
    half = keep_ref.shape[2]
    early = core_ref[0] == 0
    for i, copy in enumerate(copies):
        copy.wait()
        mixed = jnp.dot(head, block_refs[i], preferred_element_type=jnp.float32)
        mixed = mixed.astype(jnp.bfloat16)
        keep_ref[i] = jnp.where(early, mixed[:, :half], mixed[:, half:])
        give_ref[i] = jnp.where(early, mixed[:, half:], mixed[:, :half])


def finish(own, received, tail, value_up, out_proj, core, order):
    heads, width, value_width = value_up.shape
    req_rows = own.shape[0] // heads
    vmem = pl.BlockSpec(memory_space=pltpu.VMEM)
    smem = pl.BlockSpec(memory_space=pltpu.SMEM)
    chips = order.shape[0]
    half = jax.ShapeDtypeStruct((chips, req_rows, out_proj.shape[1] // (2 * chips)), jnp.bfloat16)
    return pl.pallas_call(
        functools.partial(finish_kernel, width),
        in_specs=[smem, smem, vmem, vmem, vmem, vmem, pl.BlockSpec(memory_space=pl.ANY)],
        out_specs=(vmem, vmem),
        out_shape=(half, half),
        scratch_shapes=[
            pltpu.VMEM((req_rows, heads * value_width), jnp.bfloat16),
            pltpu.VMEM((req_rows, heads, width), jnp.float32),
            pltpu.VMEM((chips, out_proj.shape[0], out_proj.shape[1] // chips), jnp.bfloat16),
            pltpu.SemaphoreType.DMA((chips,)),
        ],
        compiler_params=pltpu.CompilerParams(vmem_limit_bytes=VMEM),
        cost_estimate=COST,
        name="finish",
    )(core, order, own, received, tail, value_up, out_proj)


def on_device(
    queries, prefix_latent, tail_latent, tail_length, slot_request, key_absorb, value_up, out_proj
):
    heads_here, nope_width, latent_width = key_absorb.shape
    value_width = value_up.shape[2]
    req_rows = slot_request.shape[0]
    features = prefix_latent.shape[1]
    rope_width = features - latent_width
    exponent_scale = math.log2(math.e) / math.sqrt(nope_width + rope_width)
    core = lax.axis_index("core")
    core_at = core.reshape(1)
    z_high, y_at = lax.axis_index("z_hi"), lax.axis_index("y")
    high_size, y_size = lax.axis_size("z_hi"), lax.axis_size("y")
    chips = high_size * y_size
    devices = chips * 2
    device = (z_high * y_size + y_at) * 2 + core
    slots = -(-req_rows // devices)
    span = tail_latent.shape[1]

    def ring(value, axis, by):
        size = lax.axis_size(axis)
        return lax.ppermute(value, axis, [(i, (i + by) % size) for i in range(size)])

    def other_core(value):
        return lax.ppermute(value, "core", [(0, 1), (1, 0)])

    def z_ring(value, by):
        low, high = lax.axis_size("z_lo"), lax.axis_size("z_hi")
        size = low * high
        place = lambda z: (z % low) * high + z // low
        pairs = [(place(z), place((z + by) % size)) for z in range(size)]
        return lax.ppermute(value, ("z_lo", "z_hi"), pairs)

    def exchange(value):
        return lax.all_to_all(value, ("z_hi", "y", "core"), 0, 0, tiled=True)

    def chip_shift(value, by_high, by_y):
        place = lambda z, y: (z % high_size) * y_size + y % y_size
        pairs = [
            (place(z, y), place(z + by_high, y + by_y))
            for z in range(high_size)
            for y in range(y_size)
        ]
        return lax.ppermute(value, ("z_hi", "y"), pairs)

    picked = jnp.take(queries, slot_request, axis=0).reshape(
        req_rows, heads_here, nope_width + rope_width
    )
    query_latent = jnp.einsum(
        "rhn,hnl->rhl", picked[:, :, :nope_width], key_absorb, preferred_element_type=jnp.float32
    ).astype(jnp.bfloat16)
    query_full = jnp.concatenate([query_latent, picked[:, :, nope_width:]], axis=2)
    query_rows = query_full.reshape(req_rows * heads_here, features)

    columns = ("z_lo", "z_hi", "y")
    copies = math.prod(lax.axis_size(name) for name in columns)
    held = lax.all_to_all(
        jnp.broadcast_to(prefix_latent[None], (copies, *prefix_latent.shape)), columns, 0, 0
    )
    joined = jnp.pad(
        jnp.concatenate([tail_latent, query_full], axis=1),
        ((0, slots * devices - req_rows), (0, 0), (0, 0)),
    )
    query_rows, joined = lax.optimization_barrier((query_rows, joined))
    query_other = other_core(query_rows)
    both = jnp.concatenate([query_rows, query_other], axis=0)
    both, held, joined = lax.optimization_barrier((both, held, joined))
    held = held.reshape(2, -1, features)
    held = [held[0].T, held[1].T]

    right = [ring(half, "x", 1) for half in held]
    left = [ring(half, "x", -1) for half in held]

    joined = exchange(joined).reshape(devices, slots, span + heads_here, features)
    length = lax.dynamic_slice_in_dim(
        jnp.pad(tail_length, (0, slots * devices - req_rows), constant_values=1),
        device * slots,
        slots,
    )

    go = functools.partial(attend, width=latent_width, exponent_scale=exponent_scale)
    state = go(both, held, None, False)
    near = [right[0], left[1]]
    near, state = lax.optimization_barrier((near, state))
    far = [ring(near[0], "x", 1), ring(near[1], "x", -1)]

    state = go(both, near, state, False)
    joined, state = lax.optimization_barrier((joined, state))
    tail_part = attend_tails(joined, span, length, latent_width, exponent_scale)
    tail_part, state = lax.optimization_barrier((tail_part, state))
    late = [right[1], left[0]] + far
    tail_part = exchange(tail_part.reshape(devices * slots, heads_here, latent_width + 128))
    tail_part = tail_part.reshape(devices * slots * heads_here, latent_width + 128)

    packed_other = go(query_other, late, state, True, second=True)
    received = other_core(packed_other)
    packed_own = go(query_rows, late, state, True)

    moves = [(by_y, by_high) for by_y in (1, 2, 3, 0) for by_high in range(high_size)]
    order = jnp.stack(
        [
            ((z_high + by_high) % high_size) * y_size + (y_at + by_y) % y_size
            for by_y, by_high in moves
        ]
    ).astype(jnp.int32)
    keep, give = finish(packed_own, received, tail_part, value_up, out_proj, core_at, order)
    given = other_core(give)
    sums = [
        (keep[at : at + high_size].astype(jnp.float32) + given[at : at + high_size].astype(jnp.float32))
        for at in range(0, chips, high_size)
    ]
    total = sums[-1]
    for by_y, value in zip((1, 2, 3), sums[:-1]):
        total += ring(value.astype(jnp.bfloat16), "y", by_y).astype(jnp.float32)
    passed = ring(total[1].astype(jnp.bfloat16), "z_hi", 1)
    return (total[0] + passed.astype(jnp.float32)).astype(jnp.bfloat16)


def solution(mesh):
    fine = Mesh(
        mesh.devices.reshape(4, 2, 2, 4, 2), ("x", "z_lo", "z_hi", "y", "core")
    )
    group, seq = ("x", "z_lo"), ("z_hi", "y", "core")
    placed = (
        P(None, seq),
        P(group + seq, None),
        P(group, seq, None),
        P(group),
        P(group),
        P(seq, None, None),
        P(seq, None, None),
        P(seq, None),
    )
    return jax.shard_map(
        on_device, mesh=fine, in_specs=placed, out_specs=P(group, seq), check_vma=False
    )
```
